32 devices in a mesh: groups: 2 (over y), rows: 16 (over z, x, core).
Axes of the slice: x: 2, y: 2, z: 4, core: 2. Of those that a mesh axis runs over, the one named last changes fastest.
Arguments:
- hidden: bfloat16 [2, 4096, 8192], P(None, ('groups', 'rows')), parts along dimension 1, may hold values from -6 to 6
- q_base: bfloat16 [2, 4096, 768], P(None, ('groups', 'rows')), parts along dimension 1, may hold values from -22 to 22
- kv_base: bfloat16 [2, 4096, 256], P(None, ('groups', 'rows')), parts along dimension 1, may hold values from -6 to 6
- cache: bfloat16 [4096, 64, 256], P(('groups', 'rows')), parts along dimension 0, may hold values from -6 to 6
- lengths: int32 [4096], P(('groups', 'rows')), parts along dimension 0, may hold values from 2 to 64
- tenant: int32 [4096], P(('groups', 'rows')), parts along dimension 0, may hold values from 0 to 15, as said below
- slot_of_tenant: int32 [32], P('groups'), parts along dimension 0, may hold values from 0 to 15, each once
- bank_down: bfloat16 [32, 8192, 128], P(('groups', 'rows')), parts along dimension 0, may hold values from -0.0625 to 0.0625
- adapter_query_up_stack: bfloat16 [32, 64, 768], P(('groups', 'rows')), parts along dimension 0, may hold values from -0.75 to 0.75
- adapter_key_up_stack: bfloat16 [32, 64, 128], P(('groups', 'rows')), parts along dimension 0, may hold values from -0.75 to 0.75
Outputs:
- attended: bfloat16 [2, 4096, 768], P(None, ('groups', 'rows')), parts along dimension 1
The draws below stay inside these ranges and needn't reach their ends.
There are 2 independent parts, one for each index of `groups`. The reference program is written for one: setup_inputs(seed, part) draws one part's arguments, and reference() takes and returns one part's arrays. A program takes and returns all parts, laid end to end along the dimension named above; each array names one. Nothing has to cross between parts.
Inputs may be any that keep to these rules, and one draw needn't show every extreme that they name: The rows of one device name one tenant at most 16 times; in every draw one tenant is named exactly 16 times by the rows of every device.
All inputs are finite; a program needn't handle non-finite values.
Results may differ from the reference program's by a relative error of at most 0.0077.
Values may be sent and summed in bfloat16 or wider, within the bound.
A program may use at most 128 MiB of HBM per device.

```python
import math
import jax
import jax.numpy as jnp
from jax import lax

D = 8192
HEAD_DIM = 128
GROUP_HEADS = 6
RANK = 64
STEPS = 2
ROWS_DEV = 128
CACHE = 64
ROWS = 2048
TENANTS = 16
CAP = 16


def drawn_keys(key):
    return jax.random.rademacher(jax.random.fold_in(key, 101), (ROWS, HEAD_DIM), jnp.float32)


def draw_q_base(key, part):
    key = jax.random.fold_in(key, 5)
    draw_shape = (STEPS, ROWS, GROUP_HEADS * HEAD_DIM)
    base_draw = jnp.clip(jax.random.normal(key, draw_shape, jnp.float32), -6.0, 6.0)
    return base_draw.astype(jnp.bfloat16)


def draw_cache(key, part):
    common = drawn_keys(key)
    key = jax.random.fold_in(key, 7)
    draw_shape = (ROWS, CACHE, 2 * HEAD_DIM)
    cache_draw = jnp.clip(jax.random.normal(key, draw_shape, jnp.float32), -6.0, 6.0)
    cache_draw = cache_draw.at[:, 0, :HEAD_DIM].set(common)
    return cache_draw.astype(jnp.bfloat16)


def draw_tenant(key, part):
    key = jax.random.fold_in(key, 3)
    key_hot, key_blocks = jax.random.split(key)
    hot_tenant = jax.random.randint(key_hot, (), 0, TENANTS, dtype=jnp.int32)
    candidates_base = jnp.tile(jnp.arange(TENANTS, dtype=jnp.int32), CAP)

    def tenant_block(block_key):
        key_pool, key_mix = jax.random.split(block_key)
        candidates = jax.random.permutation(key_pool, candidates_base)
        ordering = jnp.argsort((candidates == hot_tenant).astype(jnp.int32), stable=True)
        others = candidates[ordering][:ROWS_DEV - CAP]
        block_ids = jnp.concatenate([jnp.full((CAP,), hot_tenant, jnp.int32), others])
        return jax.random.permutation(key_mix, block_ids)
    return jax.vmap(tenant_block)(jax.random.split(key_blocks, ROWS // ROWS_DEV)).reshape(ROWS)


def set_ends(entries, key, low, top_value):
    place = [jax.random.randint(jax.random.fold_in(key, axis), (), 0, length) for axis, length in enumerate(entries.shape)]
    main_axis = entries.shape.index(max(entries.shape))
    beside = place[:main_axis] + [(place[main_axis] + 1) % entries.shape[main_axis]] + place[main_axis + 1:]
    return entries.at[tuple(place)].set(low).at[tuple(beside)].set(top_value)


def levels(rng, dims, shards, smallest, top_value):
    def one(position, blocks):
        draws = jax.random.uniform(jax.random.fold_in(jax.random.fold_in(rng, 6), position), (blocks,), jnp.float32, smallest / len(shards), top_value / len(shards))
        return jnp.repeat(jnp.exp(draws), dims[position] // blocks).reshape((-1,) + (1,) * (len(dims) - position - 1))

    level = one(*shards[0])
    for cut in shards[1:]:
        level = level * one(*cut)
    return level


def centred(stream_key, dims, spread, most, shards=(), kind=jnp.bfloat16):
    entries = jax.random.normal(stream_key, dims, jnp.float32) * spread
    if len(shards) > 0:
        entries = levels(stream_key, dims, shards, -0.22, 0.18) * entries
    return jnp.clip(entries, min=-most, max=most).astype(kind)


def setup_inputs(seed: int = 0, part: int = 0) -> dict:
    arg_keys = jax.random.split(jax.random.key(seed), 11)
    own_keys = jax.random.split(jax.random.fold_in(arg_keys[10], part), 11)
    return {
        "hidden": centred(own_keys[0], (STEPS, ROWS, D), 1.0, 6.0, ((1, 16),)),
        "q_base": draw_q_base(jax.random.fold_in(jax.random.fold_in(arg_keys[10], part), 71), part),
        "kv_base": centred(own_keys[2], (STEPS, ROWS, 2 * HEAD_DIM), 1.0, 6.0, ((1, 16),)),
        "cache": draw_cache(jax.random.fold_in(jax.random.fold_in(arg_keys[10], part), 71), part),
        "lengths": set_ends(jax.random.randint(own_keys[4], (ROWS,), 2, CACHE + 1), jax.random.fold_in(own_keys[4], 1), 2, CACHE).astype(jnp.int32),
        "tenant": draw_tenant(jax.random.fold_in(jax.random.fold_in(arg_keys[10], part), 71), part),
        "slot_of_tenant": jax.random.permutation(own_keys[6], TENANTS).astype(jnp.int32),
        "bank_down": centred(own_keys[7], (TENANTS, D, 2 * RANK), D ** -0.5, 0.0625, ((0, 16),)),
        "adapter_query_up_stack": centred(own_keys[8], (TENANTS, RANK, GROUP_HEADS * HEAD_DIM), RANK ** -0.5, 0.75, ((0, 16),)),
        "adapter_key_up_stack": centred(own_keys[9], (TENANTS, RANK, HEAD_DIM), RANK ** -0.5, 0.75, ((0, 16),)),
    }


NEG = -1e+30

def attend(query, new_key, new_value, cache_keys, cache_values, length_block):
    steps_n, block_rows, width_q = query.shape
    head_dim = cache_keys.shape[2]
    head_count = width_q // head_dim
    positions_n = cache_keys.shape[1]
    score_scale = 1.0 / math.sqrt(head_dim)
    query_heads = query.astype(jnp.float32).reshape(steps_n, block_rows, head_count, head_dim)
    scores = jnp.einsum('sbgh,bch->sbgc', query_heads, cache_keys.astype(jnp.float32), precision=lax.Precision.HIGHEST) * score_scale
    in_cache = jnp.arange(positions_n, dtype=jnp.int32)[None, :] < length_block[:, None]
    scores = jnp.where(in_cache[None, :, None, :], scores, NEG)
    own_scores = jnp.einsum('sbgh,tbh->sbgt', query_heads, new_key.astype(jnp.float32), precision=lax.Precision.HIGHEST) * score_scale
    causal = jnp.arange(steps_n)[None, :] <= jnp.arange(steps_n)[:, None]
    own_scores = jnp.where(causal[:, None, None, :], own_scores, NEG)
    joined = jnp.concatenate([scores, own_scores], axis=-1)
    row_max = lax.optimization_barrier(jnp.max(joined, axis=-1, keepdims=True))
    exponent = jnp.exp(joined - row_max)
    weights = (exponent / lax.optimization_barrier(jnp.sum(exponent, axis=-1, keepdims=True))).astype(jnp.bfloat16)
    weight_wide = weights.astype(jnp.float32)
    result = jnp.einsum('sbgc,bch->sbgh', weight_wide[..., :positions_n], cache_values.astype(jnp.float32), precision=lax.Precision.HIGHEST)
    result = result + jnp.einsum('sbgt,tbh->sbgh', weight_wide[..., positions_n:], new_value.astype(jnp.float32), precision=lax.Precision.HIGHEST)
    return result.reshape(steps_n, block_rows, width_q).astype(jnp.bfloat16)

def reference(hidden, q_base, kv_base, cache, lengths, tenant, slot_of_tenant, bank_down, adapter_query_up_stack, adapter_key_up_stack):
    row_slot = slot_of_tenant[tenant].astype(jnp.int32)
    head_dim = cache.shape[2] // 2
    rank_extent = adapter_query_up_stack.shape[1]
    width_q = q_base.shape[2]

    def row_block(block_index):
        first_row = (block_index * ROWS_DEV).astype(jnp.int32)
        hidden_state_block = lax.dynamic_slice_in_dim(hidden, first_row, ROWS_DEV, 1)
        base_query = lax.dynamic_slice_in_dim(q_base, first_row, ROWS_DEV, 1)
        base_kv = lax.dynamic_slice_in_dim(kv_base, first_row, ROWS_DEV, 1)
        cache_block = lax.dynamic_slice_in_dim(cache, first_row, ROWS_DEV, 0)
        length_block = lax.dynamic_slice_in_dim(lengths, first_row, ROWS_DEV, 0)
        tenant_own_slot = lax.dynamic_slice_in_dim(row_slot, first_row, ROWS_DEV, 0)
        down_projected = bank_down[tenant_own_slot].astype(jnp.float32)
        reduced_rank_input = jnp.einsum('uym,ymz->uyz', hidden_state_block.astype(jnp.float32), down_projected, precision=lax.Precision.HIGHEST).astype(jnp.bfloat16)
        reduced_rank_wide = reduced_rank_input.astype(jnp.float32)
        query_correction = jnp.einsum('zdc,dce->zde', reduced_rank_wide[..., :rank_extent], adapter_query_up_stack[tenant_own_slot].astype(jnp.float32), precision=lax.Precision.HIGHEST).astype(jnp.bfloat16)
        key_correction = jnp.einsum('zdc,dce->zde', reduced_rank_wide[..., rank_extent:], adapter_key_up_stack[tenant_own_slot].astype(jnp.float32), precision=lax.Precision.HIGHEST).astype(jnp.bfloat16)
        query = (base_query.astype(jnp.float32) + query_correction.astype(jnp.float32)).astype(jnp.bfloat16)
        new_key = (base_kv[..., :head_dim].astype(jnp.float32) + key_correction.astype(jnp.float32)).astype(jnp.bfloat16)
        new_value = base_kv[..., head_dim:]
        return attend(query, new_key, new_value, cache_block[..., :head_dim], cache_block[..., head_dim:], length_block)
    blocks_out = lax.map(row_block, jnp.arange(ROWS // ROWS_DEV, dtype=jnp.int32))
    return jnp.transpose(blocks_out, (1, 0, 2, 3)).reshape(STEPS, ROWS, width_q)
```

```python
import functools
import math

import jax
import jax.numpy as jnp
from jax import lax
from jax.experimental import pallas as pl
from jax.experimental.pallas import tpu as pltpu
from jax.sharding import PartitionSpec as P

NEG = -1e30


def attend(query, new_key, new_value, cache_keys, cache_values, length_block):
    steps_n, block_rows, width_q = query.shape
    head_dim = cache_keys.shape[2]
    head_count = width_q // head_dim
    positions_n = cache_keys.shape[1]
    score_scale = 1.0 / math.sqrt(head_dim)
    query_heads = query.reshape(steps_n, block_rows, head_count, head_dim)
    scores = (
        jnp.einsum("sbgh,bch->sbgc", query_heads, cache_keys, preferred_element_type=jnp.float32)
        * score_scale
    )
    in_cache = jnp.arange(positions_n, dtype=jnp.int32)[None, :] < length_block[:, None]
    scores = jnp.where(in_cache[None, :, None, :], scores, NEG)
    own_scores = (
        jnp.einsum("sbgh,tbh->sbgt", query_heads, new_key, preferred_element_type=jnp.float32)
        * score_scale
    )
    causal = jnp.arange(steps_n)[None, :] <= jnp.arange(steps_n)[:, None]
    own_scores = jnp.where(causal[:, None, None, :], own_scores, NEG)
    joined = jnp.concatenate([scores, own_scores], axis=-1)
    row_max = jnp.max(joined, axis=-1, keepdims=True)
    exponent = jnp.exp(joined - row_max)
    weights = (exponent / jnp.sum(exponent, axis=-1, keepdims=True)).astype(jnp.bfloat16)
    result = jnp.einsum(
        "sbgc,bch->sbgh",
        weights[..., :positions_n],
        cache_values,
        preferred_element_type=jnp.float32,
    )
    result = result + jnp.einsum(
        "sbgt,tbh->sbgh", weights[..., positions_n:], new_value, preferred_element_type=jnp.float32
    )
    return result.reshape(steps_n, block_rows, width_q).astype(jnp.bfloat16)


def flipped(index, mask, bits):
    result = 0
    for bit in range(bits):
        value = (index // (1 << bit)) % 2
        if (mask >> bit) & 1:
            value = 1 - value
        result = result + value * (1 << bit)
    return result


def low_rank_kernel(
    bits,
    hidden_ref,
    bank_ref,
    slot_ref,
    out_ref,
    x_ref,
    w_ref,
    s_ref,
    total_ref,
    part_ref,
    back_ref,
    local_sem,
    hidden_send,
    hidden_recv,
    slot_send,
    slot_recv,
    bank_send,
    bank_recv,
    part_send,
    part_recv,
):
    peers = 1 << bits
    half = peers // 2
    steps_n, rows_here, width = hidden_ref.shape
    chunk = width // half
    rank2 = bank_ref.shape[2]
    me = lax.axis_index("rows")
    mine = me % half

    def hidden_source(index):
        return hidden_ref.at[:, :, pl.ds(pl.multiple_of(index * chunk, chunk), chunk)]

    def bank_source(index):
        return bank_ref.at[0, pl.ds(pl.multiple_of(index * chunk, chunk), chunk), :]

    own_hidden = pltpu.make_async_copy(hidden_source(mine), x_ref.at[0], local_sem.at[0])
    own_bank = pltpu.make_async_copy(
        bank_source(mine), w_ref.at[:, pl.ds(0, rank2)], local_sem.at[1]
    )
    own_hidden.start()
    own_bank.start()
    s_ref[0] = slot_ref[...]

    barrier = pltpu.get_barrier_semaphore()
    for mask in range(1, peers):
        pl.semaphore_signal(
            barrier,
            inc=1,
            device_id={"rows": flipped(me, mask, bits)},
            device_id_type=pl.DeviceIdType.MESH,
        )
    pl.semaphore_wait(barrier, peers - 1)

    def remote(source, target, send, recv, mask):
        return pltpu.make_async_remote_copy(
            src_ref=source,
            dst_ref=target,
            send_sem=send.at[mask],
            recv_sem=recv.at[mask],
            device_id={"rows": flipped(me, mask, bits)},
            device_id_type=pl.DeviceIdType.MESH,
        )

    sends = []
    hidden_copies = {}
    slot_copies = {}
    bank_copies = {}
    part_copies = {}
    for mask in range(half - 1, 0, -1):
        hidden_copies[mask] = remote(
            hidden_source(flipped(mine, mask, bits - 1)),
            x_ref.at[mask],
            hidden_send,
            hidden_recv,
            mask,
        )
        slot_copies[mask] = remote(slot_ref, s_ref.at[mask], slot_send, slot_recv, mask)
        hidden_copies[mask].start()
        slot_copies[mask].start()
        sends += [hidden_copies[mask], slot_copies[mask]]
    for mask in range(1, peers):
        bank_copies[mask] = remote(
            bank_source(flipped(mine, mask % half, bits - 1)),
            w_ref.at[:, pl.ds(mask * rank2, rank2)],
            bank_send,
            bank_recv,
            mask,
        )
        bank_copies[mask].start()
        sends.append(bank_copies[mask])

    total_ref[...] = jnp.zeros_like(total_ref)
    own_hidden.wait()
    own_bank.wait()
    for mask in range(1, half):
        hidden_copies[mask].wait_recv()
        slot_copies[mask].wait_recv()
    for first in range(0, peers, 2):
        for mask in (first, first + 1):
            if mask:
                bank_copies[mask].wait_recv()
        owner_a = flipped(me, first, bits)
        owner_b = flipped(me, first + 1, bits)

        def multiply(source, carry, first=first, owner_a=owner_a, owner_b=owner_b):
            rows = x_ref[source].reshape(steps_n * rows_here, chunk)
            product = jnp.dot(
                rows,
                w_ref[:, first * rank2 : (first + 2) * rank2],
                preferred_element_type=jnp.float32,
            ).reshape(steps_n, rows_here, 2 * rank2)
            slots = s_ref[source][None]
            total_ref[source] = jnp.where(
                slots == owner_a,
                product[..., :rank2],
                jnp.where(slots == owner_b, product[..., rank2:], total_ref[source]),
            )
            return carry

        lax.fori_loop(0, half, multiply, 0)

    part_ref[...] = total_ref[...].astype(jnp.bfloat16)
    for mask in range(1, half):
        part_copies[mask] = remote(
            part_ref.at[mask], back_ref.at[mask], part_send, part_recv, mask
        )
        part_copies[mask].start()
        sends.append(part_copies[mask])
    result = total_ref[0]
    for mask in range(1, half):
        part_copies[mask].wait_recv()
        result = result + back_ref[mask].astype(jnp.float32)
    out_ref[...] = result.astype(jnp.bfloat16)
    for copy in sends:
        copy.wait_send()


def low_rank_call(hidden, bank_down, slots, peers):
    bits = peers.bit_length() - 1
    half = peers // 2
    steps_n, rows_here, width = hidden.shape
    chunk = width // half
    rank2 = bank_down.shape[2]
    dma = pltpu.SemaphoreType.DMA
    return pl.pallas_call(
        functools.partial(low_rank_kernel, bits),
        out_shape=jax.ShapeDtypeStruct((steps_n, rows_here, rank2), jnp.bfloat16),
        in_specs=[
            pl.BlockSpec(memory_space=pl.ANY),
            pl.BlockSpec(memory_space=pl.ANY),
            pl.BlockSpec(memory_space=pltpu.VMEM),
        ],
        out_specs=pl.BlockSpec(memory_space=pltpu.VMEM),
        scratch_shapes=[
            pltpu.VMEM((half, steps_n, rows_here, chunk), jnp.bfloat16),
            pltpu.VMEM((chunk, peers * rank2), jnp.bfloat16),
            pltpu.VMEM((half, rows_here, rank2), jnp.int32),
            pltpu.VMEM((half, steps_n, rows_here, rank2), jnp.float32),
            pltpu.VMEM((half, steps_n, rows_here, rank2), jnp.bfloat16),
            pltpu.VMEM((half, steps_n, rows_here, rank2), jnp.bfloat16),
            dma((2,)),
            dma((half,)),
            dma((half,)),
            dma((half,)),
            dma((half,)),
            dma((peers,)),
            dma((peers,)),
            dma((half,)),
            dma((half,)),
        ],
        compiler_params=pltpu.CompilerParams(
            collective_id=0, has_side_effects=True, vmem_limit_bytes=40 * 1024 * 1024
        ),
        cost_estimate=pl.CostEstimate(
            flops=2 * half * steps_n * rows_here * chunk * peers * rank2,
            bytes_accessed=16 * 1024 * 1024,
            transcendentals=0,
        ),
    )(hidden, bank_down, slots)


def split_width(
    hidden,
    q_base,
    kv_base,
    cache,
    lengths,
    tenant,
    slot_of_tenant,
    bank_down,
    adapter_query_up_stack,
    adapter_key_up_stack,
):
    peers = lax.axis_size("rows")
    steps_n, rows_here, _ = hidden.shape
    head_dim = cache.shape[2] // 2
    width_q = q_base.shape[2]
    rank = adapter_query_up_stack.shape[1]
    tenant_ids = jnp.arange(slot_of_tenant.shape[0], dtype=jnp.int32)
    owner = jnp.sum(
        jnp.where(tenant[:, None] == tenant_ids[None, :], slot_of_tenant[None, :], 0), axis=1
    )
    ups = jnp.concatenate([adapter_query_up_stack[0], adapter_key_up_stack[0]], axis=1)
    ups = lax.all_gather(ups, "rows", axis=0, tiled=True)
    slots = jnp.broadcast_to(owner[:, None], (rows_here, 2 * rank)).astype(jnp.int32)
    low_rank = low_rank_call(hidden, bank_down, slots, peers)
    chosen = owner[:, None] == jnp.arange(peers, dtype=jnp.int32)[None, :]

    def correction(part, up):
        placed = jnp.where(chosen[None, :, :, None], part[:, :, None, :], 0)
        placed = placed.reshape(steps_n * rows_here, peers * rank).astype(jnp.bfloat16)
        product = jnp.dot(placed, up, preferred_element_type=jnp.float32).astype(jnp.bfloat16)
        return product.astype(jnp.float32).reshape(steps_n, rows_here, up.shape[1])

    delta_q = correction(low_rank[..., :rank], ups[:, :width_q])
    delta_k = correction(low_rank[..., rank:], ups[:, width_q:])
    query = (q_base.astype(jnp.float32) + delta_q).astype(jnp.bfloat16)
    new_key = (kv_base[..., :head_dim].astype(jnp.float32) + delta_k).astype(jnp.bfloat16)
    new_value = kv_base[..., head_dim:]
    return attend(query, new_key, new_value, cache[..., :head_dim], cache[..., head_dim:], lengths)


def local(
    hidden,
    q_base,
    kv_base,
    cache,
    lengths,
    tenant,
    slot_of_tenant,
    bank_down,
    adapter_query_up_stack,
    adapter_key_up_stack,
):
    peer_count = lax.axis_size("rows")
    steps_n, rows_here, model_width = hidden.shape
    capacity = max(2, (2 * rows_here + peer_count - 1) // peer_count)
    tenant_count = slot_of_tenant.shape[0]
    head_dim = cache.shape[2] // 2
    width_q = q_base.shape[2]
    rank_extent = adapter_query_up_stack.shape[1]
    tenant_ids = jnp.arange(tenant_count, dtype=jnp.int32)
    owner_dev = jnp.sum(
        jnp.where(tenant[:, None] == tenant_ids[None, :], slot_of_tenant[None, :], 0), axis=1
    )
    positions = jnp.arange(rows_here, dtype=jnp.int32)
    earlier = (tenant[:, None] == tenant[None, :]) & (positions[None, :] < positions[:, None])
    slot_column = owner_dev * capacity + jnp.sum(earlier.astype(jnp.int32), axis=1)
    placing = (
        slot_column[:, None] == jnp.arange(peer_count * capacity, dtype=jnp.int32)[None, :]
    ).astype(jnp.bfloat16)
    down_projected = bank_down[0]
    up_query = adapter_query_up_stack[0]
    up_key = adapter_key_up_stack[0]
    collected = []
    for step_index in range(steps_n):
        outgoing = jnp.einsum(
            "bc,bd->cd", placing, hidden[step_index], preferred_element_type=jnp.float32
        ).astype(jnp.bfloat16)
        outgoing = outgoing.reshape(peer_count, capacity, model_width)
        received = lax.all_to_all(outgoing, "rows", split_axis=0, concat_axis=0, tiled=True)
        flattened = received.reshape(-1, model_width)
        reduced_rank_input = jnp.dot(
            flattened, down_projected, preferred_element_type=jnp.float32
        ).astype(jnp.bfloat16)
        query_correction = jnp.dot(
            reduced_rank_input[:, :rank_extent], up_query, preferred_element_type=jnp.float32
        ).astype(jnp.bfloat16)
        key_correction = jnp.dot(
            reduced_rank_input[:, rank_extent:], up_key, preferred_element_type=jnp.float32
        ).astype(jnp.bfloat16)
        joined_delta = jnp.concatenate([query_correction, key_correction], axis=1)
        returned = lax.all_to_all(
            joined_delta.reshape(received.shape[0], received.shape[1], width_q + head_dim),
            "rows",
            split_axis=0,
            concat_axis=0,
            tiled=True,
        )
        returned = returned.reshape(peer_count * capacity, width_q + head_dim)
        collected.append(jnp.dot(placing, returned, preferred_element_type=jnp.float32))
    deltas = jnp.stack(collected)
    query = (q_base.astype(jnp.float32) + deltas[..., :width_q]).astype(jnp.bfloat16)
    new_key = (kv_base[..., :head_dim].astype(jnp.float32) + deltas[..., width_q:]).astype(
        jnp.bfloat16
    )
    new_value = kv_base[..., head_dim:]
    return attend(query, new_key, new_value, cache[..., :head_dim], cache[..., head_dim:], lengths)


def solution(mesh):
    peers = mesh.shape["rows"]
    small = 4 <= peers <= 16 and peers & (peers - 1) == 0
    return jax.shard_map(
        split_width if small else local,
        mesh=mesh,
        in_specs=(
            P(None, ("groups", "rows"), None),
            P(None, ("groups", "rows"), None),
            P(None, ("groups", "rows"), None),
            P(("groups", "rows"), None, None),
            P(("groups", "rows")),
            P(("groups", "rows")),
            P("groups"),
            P(("groups", "rows"), None, None),
            P(("groups", "rows"), None, None),
            P(("groups", "rows"), None, None),
        ),
        out_specs=P(None, ("groups", "rows"), None),
        check_vma=False,
    )
```

```python
import functools
import math

import jax
import jax.numpy as jnp
from jax import lax
from jax.experimental import pallas as pl
from jax.experimental.pallas import tpu as pltpu
from jax.sharding import PartitionSpec as P

NEG = -1e30


def attend(query, new_key, new_value, cache_keys, cache_values, length_block):
    steps_n, block_rows, width_q = query.shape
    head_dim = cache_keys.shape[2]
    head_count = width_q // head_dim
    positions_n = cache_keys.shape[1]
    score_scale = 1.0 / math.sqrt(head_dim)
    query_heads = query.reshape(steps_n, block_rows, head_count, head_dim)
    scores = (
        jnp.einsum("sbgh,bch->sbgc", query_heads, cache_keys, preferred_element_type=jnp.float32)
        * score_scale
    )
    in_cache = jnp.arange(positions_n, dtype=jnp.int32)[None, :] < length_block[:, None]
    scores = jnp.where(in_cache[None, :, None, :], scores, NEG)
    own_scores = (
        jnp.einsum("sbgh,tbh->sbgt", query_heads, new_key, preferred_element_type=jnp.float32)
        * score_scale
    )
    causal = jnp.arange(steps_n)[None, :] <= jnp.arange(steps_n)[:, None]
    own_scores = jnp.where(causal[:, None, None, :], own_scores, NEG)
    joined = jnp.concatenate([scores, own_scores], axis=-1)
    row_max = jnp.max(joined, axis=-1, keepdims=True)
    exponent = jnp.exp(joined - row_max)
    weights = (exponent / jnp.sum(exponent, axis=-1, keepdims=True)).astype(jnp.bfloat16)
    result = jnp.einsum(
        "sbgc,bch->sbgh",
        weights[..., :positions_n],
        cache_values,
        preferred_element_type=jnp.float32,
    )
    result = result + jnp.einsum(
        "sbgt,tbh->sbgh", weights[..., positions_n:], new_value, preferred_element_type=jnp.float32
    )
    return result.reshape(steps_n, block_rows, width_q).astype(jnp.bfloat16)


def flipped(index, mask, bits):
    result = 0
    for bit in range(bits):
        value = (index // (1 << bit)) % 2
        if (mask >> bit) & 1:
            value = 1 - value
        result = result + value * (1 << bit)
    return result


def low_rank_kernel(
    bits,
    hidden_ref,
    bank_ref,
    slot_ref,
    out_ref,
    x_ref,
    w_ref,
    s_ref,
    column_ref,
    total_ref,
    part_ref,
    back_ref,
    local_sem,
    hidden_send,
    hidden_recv,
    slot_send,
    slot_recv,
    bank_send,
    bank_recv,
    part_send,
    part_recv,
):
    peers = 1 << bits
    half = peers // 2
    steps_n, rows_here, width = hidden_ref.shape
    chunk = width // half
    rank2 = bank_ref.shape[2]
    me = lax.axis_index("rows")
    mine = me % half
    group = 2

    def hidden_source(index):
        return hidden_ref.at[:, :, pl.ds(pl.multiple_of(index * chunk, chunk), chunk)]

    def bank_source(index):
        return bank_ref.at[0, pl.ds(pl.multiple_of(index * chunk, chunk), chunk), :]

    own_hidden = pltpu.make_async_copy(hidden_source(mine), x_ref.at[0], local_sem.at[0])
    own_bank = pltpu.make_async_copy(
        bank_source(mine), w_ref.at[0], local_sem.at[1]
    )
    own_hidden.start()
    own_bank.start()
    s_ref[0] = slot_ref[...]

    barrier = pltpu.get_barrier_semaphore()
    for mask in range(1, peers):
        pl.semaphore_signal(
            barrier,
            inc=1,
            device_id={"rows": flipped(me, mask, bits)},
            device_id_type=pl.DeviceIdType.MESH,
        )
    pl.semaphore_wait(barrier, peers - 1)

    def remote(source, target, send, recv, mask):
        return pltpu.make_async_remote_copy(
            src_ref=source,
            dst_ref=target,
            send_sem=send.at[mask],
            recv_sem=recv.at[mask],
            device_id={"rows": flipped(me, mask, bits)},
            device_id_type=pl.DeviceIdType.MESH,
        )

    hidden_copies = {}
    slot_copies = {}
    bank_copies = {}
    part_copies = {}
    for mask in range(1, half):
        hidden_copies[mask] = remote(
            hidden_source(flipped(mine, mask, bits - 1)),
            x_ref.at[mask],
            hidden_send,
            hidden_recv,
            mask,
        )
        slot_copies[mask] = remote(slot_ref, s_ref.at[mask], slot_send, slot_recv, mask)
    for mask in range(1, peers):
        bank_copies[mask] = remote(
            bank_source(flipped(mine, mask % half, bits - 1)),
            w_ref.at[mask],
            bank_send,
            bank_recv,
            mask,
        )
    sends = [*hidden_copies.values(), *slot_copies.values(), *bank_copies.values()]
    for mask in range(half - 1, 0, -1):
        hidden_copies[mask].start()
        slot_copies[mask].start()
    for mask in range(1, peers):
        bank_copies[mask].start()
    total_ref[...] = jnp.zeros_like(total_ref)
    own_hidden.wait()
    own_bank.wait()
    for mask in range(1, half):
        hidden_copies[mask].wait_recv()
        slot_copies[mask].wait_recv()
    for mask in range(half):
        column_ref[mask] = jnp.broadcast_to(s_ref[mask][:1], (rank2, rows_here)).T
    for first in range(0, peers, 2):
        for mask in (first, first + 1):
            if mask:
                bank_copies[mask].wait_recv()
        owner_a = flipped(me, first, bits)
        owner_b = flipped(me, first + 1, bits)

        def multiply(source, carry, first=first, owner_a=owner_a, owner_b=owner_b):
            some = pl.ds(source * group, group)
            product = jnp.dot(
                x_ref[some].reshape(group * steps_n * rows_here, chunk),
                jnp.concatenate([w_ref[first], w_ref[first + 1]], axis=1),
                preferred_element_type=jnp.float32,
            ).reshape(group, steps_n, rows_here, 2 * rank2)
            slots = column_ref[some][:, None]
            total_ref[some] = jnp.where(
                slots == owner_a,
                product[..., :rank2],
                jnp.where(slots == owner_b, product[..., rank2:], total_ref[some]),
            )
            return carry

        if first != peers - 2:
            lax.fori_loop(0, half // group, multiply, 0)
            continue
        for block in reversed(range(half // group)):
            multiply(block, 0)
            for mask in range(block * group, (block + 1) * group):
                if mask:
                    part_ref[mask] = total_ref[mask].astype(jnp.bfloat16)
                    part_copies[mask] = remote(
                        part_ref.at[mask], back_ref.at[mask], part_send, part_recv, mask
                    )
                    part_copies[mask].start()
                    sends.append(part_copies[mask])

    result = total_ref[0]
    for mask in range(1, half):
        part_copies[mask].wait_recv()
        result = result + back_ref[mask].astype(jnp.float32)
    out_ref[...] = result.astype(jnp.bfloat16)
    for copy in sends:
        copy.wait_send()


def low_rank_call(hidden, bank_down, slots, peers):
    bits = peers.bit_length() - 1
    half = peers // 2
    steps_n, rows_here, width = hidden.shape
    chunk = width // half
    rank2 = bank_down.shape[2]
    dma = pltpu.SemaphoreType.DMA
    return pl.pallas_call(
        functools.partial(low_rank_kernel, bits),
        out_shape=jax.ShapeDtypeStruct((steps_n, rows_here, rank2), jnp.bfloat16),
        in_specs=[
            pl.BlockSpec(memory_space=pl.ANY),
            pl.BlockSpec(memory_space=pl.ANY),
            pl.BlockSpec(memory_space=pltpu.VMEM),
        ],
        out_specs=pl.BlockSpec(memory_space=pltpu.VMEM),
        scratch_shapes=[
            pltpu.VMEM((half, steps_n, rows_here, chunk), jnp.bfloat16),
            pltpu.VMEM((peers, chunk, rank2), jnp.bfloat16),
            pltpu.VMEM((half, *slots.shape), jnp.int32),
            pltpu.VMEM((half, rows_here, rank2), jnp.int32),
            pltpu.VMEM((half, steps_n, rows_here, rank2), jnp.float32),
            pltpu.VMEM((half, steps_n, rows_here, rank2), jnp.bfloat16),
            pltpu.VMEM((half, steps_n, rows_here, rank2), jnp.bfloat16),
            dma((2,)),
            dma((half,)),
            dma((half,)),
            dma((half,)),
            dma((half,)),
            dma((peers,)),
            dma((peers,)),
            dma((half,)),
            dma((half,)),
        ],
        compiler_params=pltpu.CompilerParams(
            collective_id=0, has_side_effects=True, vmem_limit_bytes=60 * 1024 * 1024
        ),
        cost_estimate=pl.CostEstimate(
            flops=2 * half * steps_n * rows_here * chunk * peers * rank2,
            bytes_accessed=16 * 1024 * 1024,
            transcendentals=0,
        ),
    )(hidden, bank_down, slots)


def split_width(
    hidden,
    q_base,
    kv_base,
    cache,
    lengths,
    tenant,
    slot_of_tenant,
    bank_down,
    adapter_query_up_stack,
    adapter_key_up_stack,
):
    peers = lax.axis_size("rows")
    steps_n, rows_here, _ = hidden.shape
    head_dim = cache.shape[2] // 2
    width_q = q_base.shape[2]
    rank = adapter_query_up_stack.shape[1]
    tenant_ids = jnp.arange(slot_of_tenant.shape[0], dtype=jnp.int32)
    owner = jnp.sum(
        jnp.where(tenant[:, None] == tenant_ids[None, :], slot_of_tenant[None, :], 0), axis=1
    )
    ups = jnp.concatenate([adapter_query_up_stack[0], adapter_key_up_stack[0]], axis=1)
    ups = lax.all_gather(ups, "rows", axis=0, tiled=True)
    slots = jnp.broadcast_to(owner[None, :], (8, rows_here)).astype(jnp.int32)
    low_rank = low_rank_call(hidden, bank_down, slots, peers)
    chosen = owner[:, None] == jnp.arange(peers, dtype=jnp.int32)[None, :]

    def correction(part, up):
        placed = jnp.where(chosen[None, :, :, None], part[:, :, None, :], 0)
        placed = placed.reshape(steps_n * rows_here, peers * rank).astype(jnp.bfloat16)
        product = jnp.dot(placed, up, preferred_element_type=jnp.float32).astype(jnp.bfloat16)
        return product.astype(jnp.float32).reshape(steps_n, rows_here, up.shape[1])

    delta_q = correction(low_rank[..., :rank], ups[:, :width_q])
    delta_k = correction(low_rank[..., rank:], ups[:, width_q:])
    query = (q_base.astype(jnp.float32) + delta_q).astype(jnp.bfloat16)
    new_key = (kv_base[..., :head_dim].astype(jnp.float32) + delta_k).astype(jnp.bfloat16)
    new_value = kv_base[..., head_dim:]
    return attend(query, new_key, new_value, cache[..., :head_dim], cache[..., head_dim:], lengths)


def local(
    hidden,
    q_base,
    kv_base,
    cache,
    lengths,
    tenant,
    slot_of_tenant,
    bank_down,
    adapter_query_up_stack,
    adapter_key_up_stack,
):
    peer_count = lax.axis_size("rows")
    steps_n, rows_here, model_width = hidden.shape
    capacity = max(2, (2 * rows_here + peer_count - 1) // peer_count)
    tenant_count = slot_of_tenant.shape[0]
    head_dim = cache.shape[2] // 2
    width_q = q_base.shape[2]
    rank_extent = adapter_query_up_stack.shape[1]
    tenant_ids = jnp.arange(tenant_count, dtype=jnp.int32)
    owner_dev = jnp.sum(
        jnp.where(tenant[:, None] == tenant_ids[None, :], slot_of_tenant[None, :], 0), axis=1
    )
    positions = jnp.arange(rows_here, dtype=jnp.int32)
    earlier = (tenant[:, None] == tenant[None, :]) & (positions[None, :] < positions[:, None])
    slot_column = owner_dev * capacity + jnp.sum(earlier.astype(jnp.int32), axis=1)
    placing = (
        slot_column[:, None] == jnp.arange(peer_count * capacity, dtype=jnp.int32)[None, :]
    ).astype(jnp.bfloat16)
    down_projected = bank_down[0]
    up_query = adapter_query_up_stack[0]
    up_key = adapter_key_up_stack[0]
    collected = []
    for step_index in range(steps_n):
        outgoing = jnp.einsum(
            "bc,bd->cd", placing, hidden[step_index], preferred_element_type=jnp.float32
        ).astype(jnp.bfloat16)
        outgoing = outgoing.reshape(peer_count, capacity, model_width)
        received = lax.all_to_all(outgoing, "rows", split_axis=0, concat_axis=0, tiled=True)
        flattened = received.reshape(-1, model_width)
        reduced_rank_input = jnp.dot(
            flattened, down_projected, preferred_element_type=jnp.float32
        ).astype(jnp.bfloat16)
        query_correction = jnp.dot(
            reduced_rank_input[:, :rank_extent], up_query, preferred_element_type=jnp.float32
        ).astype(jnp.bfloat16)
        key_correction = jnp.dot(
            reduced_rank_input[:, rank_extent:], up_key, preferred_element_type=jnp.float32
        ).astype(jnp.bfloat16)
        joined_delta = jnp.concatenate([query_correction, key_correction], axis=1)
        returned = lax.all_to_all(
            joined_delta.reshape(received.shape[0], received.shape[1], width_q + head_dim),
            "rows",
            split_axis=0,
            concat_axis=0,
            tiled=True,
        )
        returned = returned.reshape(peer_count * capacity, width_q + head_dim)
        collected.append(jnp.dot(placing, returned, preferred_element_type=jnp.float32))
    deltas = jnp.stack(collected)
    query = (q_base.astype(jnp.float32) + deltas[..., :width_q]).astype(jnp.bfloat16)
    new_key = (kv_base[..., :head_dim].astype(jnp.float32) + deltas[..., width_q:]).astype(
        jnp.bfloat16
    )
    new_value = kv_base[..., head_dim:]
    return attend(query, new_key, new_value, cache[..., :head_dim], cache[..., head_dim:], lengths)


def solution(mesh):
    peers = mesh.shape["rows"]
    small = 4 <= peers <= 16 and peers & (peers - 1) == 0
    return jax.shard_map(
        split_width if small else local,
        mesh=mesh,
        in_specs=(
            P(None, ("groups", "rows"), None),
            P(None, ("groups", "rows"), None),
            P(None, ("groups", "rows"), None),
            P(("groups", "rows"), None, None),
            P(("groups", "rows")),
            P(("groups", "rows")),
            P("groups"),
            P(("groups", "rows"), None, None),
            P(("groups", "rows"), None, None),
            P(("groups", "rows"), None, None),
        ),
        out_specs=P(None, ("groups", "rows"), None),
        check_vma=False,
    )
```

```python
import functools
import math

import jax
import jax.numpy as jnp
from jax import lax
from jax.experimental import pallas as pl
from jax.experimental.pallas import tpu as pltpu
from jax.sharding import PartitionSpec as P

NEG = -1e30


def attend(query, new_key, new_value, cache_keys, cache_values, length_block):
    steps_n, block_rows, width_q = query.shape
    head_dim = cache_keys.shape[2]
    head_count = width_q // head_dim
    positions_n = cache_keys.shape[1]
    score_scale = 1.0 / math.sqrt(head_dim)
    query_heads = query.reshape(steps_n, block_rows, head_count, head_dim)
    scores = (
        jnp.einsum("sbgh,bch->sbgc", query_heads, cache_keys, preferred_element_type=jnp.float32)
        * score_scale
    )
    in_cache = jnp.arange(positions_n, dtype=jnp.int32)[None, :] < length_block[:, None]
    scores = jnp.where(in_cache[None, :, None, :], scores, NEG)
    wide_heads = query_heads.astype(jnp.float32)
    own_scores = (
        jnp.stack(
            [
                jnp.sum(wide_heads * new_key[t].astype(jnp.float32)[None, :, None, :], axis=-1)
                for t in range(steps_n)
            ],
            axis=-1,
        )
        * score_scale
    )
    causal = jnp.arange(steps_n)[None, :] <= jnp.arange(steps_n)[:, None]
    own_scores = jnp.where(causal[:, None, None, :], own_scores, NEG)
    joined = jnp.concatenate([scores, own_scores], axis=-1)
    row_max = jnp.max(joined, axis=-1, keepdims=True)
    exponent = jnp.exp(joined - row_max)
    weights = (exponent / jnp.sum(exponent, axis=-1, keepdims=True)).astype(jnp.bfloat16)
    result = jnp.einsum(
        "sbgc,bch->sbgh",
        weights[..., :positions_n],
        cache_values,
        preferred_element_type=jnp.float32,
    )
    result = result + jnp.einsum(
        "sbgt,tbh->sbgh", weights[..., positions_n:], new_value, preferred_element_type=jnp.float32
    )
    return result.reshape(steps_n, block_rows, width_q).astype(jnp.bfloat16)


def flipped(index, mask, bits):
    result = 0
    for bit in range(bits):
        value = (index // (1 << bit)) % 2
        if (mask >> bit) & 1:
            value = 1 - value
        result = result + value * (1 << bit)
    return result


def low_rank_kernel(
    bits,
    hidden_ref,
    bank_ref,
    slot_ref,
    out_ref,
    x_ref,
    w_ref,
    s_ref,
    column_ref,
    total_ref,
    part_ref,
    back_ref,
    local_sem,
    hidden_send,
    hidden_recv,
    slot_send,
    slot_recv,
    bank_send,
    bank_recv,
    part_send,
    part_recv,
):
    peers = 1 << bits
    half = peers // 2
    steps_n, rows_here, width = hidden_ref.shape
    chunk = width // half
    rank2 = bank_ref.shape[2]
    me = lax.axis_index("rows")
    mine = me % half
    group = 2

    def hidden_source(index):
        return hidden_ref.at[:, :, pl.ds(pl.multiple_of(index * chunk, chunk), chunk)]

    def bank_source(index):
        return bank_ref.at[0, pl.ds(pl.multiple_of(index * chunk, chunk), chunk), :]

    own_hidden = pltpu.make_async_copy(hidden_source(mine), x_ref.at[0], local_sem.at[0])
    own_bank = pltpu.make_async_copy(
        bank_source(mine), w_ref.at[0], local_sem.at[1]
    )
    own_hidden.start()
    own_bank.start()
    s_ref[0] = slot_ref[...]

    barrier = pltpu.get_barrier_semaphore()
    for mask in range(1, peers):
        pl.semaphore_signal(
            barrier,
            inc=1,
            device_id={"rows": flipped(me, mask, bits)},
            device_id_type=pl.DeviceIdType.MESH,
        )
    pl.semaphore_wait(barrier, peers - 1)

    def remote(source, target, send, recv, mask):
        return pltpu.make_async_remote_copy(
            src_ref=source,
            dst_ref=target,
            send_sem=send.at[mask],
            recv_sem=recv.at[mask],
            device_id={"rows": flipped(me, mask, bits)},
            device_id_type=pl.DeviceIdType.MESH,
        )

    hidden_copies = {}
    slot_copies = {}
    bank_copies = {}
    part_copies = {}
    for mask in range(1, half):
        hidden_copies[mask] = remote(
            hidden_source(flipped(mine, mask, bits - 1)),
            x_ref.at[mask],
            hidden_send,
            hidden_recv,
            mask,
        )
        slot_copies[mask] = remote(slot_ref, s_ref.at[mask], slot_send, slot_recv, mask)
    for mask in range(1, peers):
        bank_copies[mask] = remote(
            bank_source(flipped(mine, mask % half, bits - 1)),
            w_ref.at[mask],
            bank_send,
            bank_recv,
            mask,
        )
    sends = [*hidden_copies.values(), *slot_copies.values(), *bank_copies.values()]
    for mask in range(half - 1, 0, -1):
        hidden_copies[mask].start()
        slot_copies[mask].start()
    for mask in range(1, peers):
        bank_copies[mask].start()
    total_ref[...] = jnp.zeros_like(total_ref)
    own_hidden.wait()
    own_bank.wait()
    for mask in range(1, half):
        hidden_copies[mask].wait_recv()
        slot_copies[mask].wait_recv()
    for mask in range(half):
        column_ref[mask] = jnp.broadcast_to(s_ref[mask][:1], (rank2, rows_here)).T
    for first in range(0, peers, 2):
        for mask in (first, first + 1):
            if mask:
                bank_copies[mask].wait_recv()
        owner_a = flipped(me, first, bits)
        owner_b = flipped(me, first + 1, bits)

        def multiply(source, carry, first=first, owner_a=owner_a, owner_b=owner_b):
            some = pl.ds(source * group, group)
            product = jnp.dot(
                x_ref[some].reshape(group * steps_n * rows_here, chunk),
                jnp.concatenate([w_ref[first], w_ref[first + 1]], axis=1),
                preferred_element_type=jnp.float32,
            ).reshape(group, steps_n, rows_here, 2 * rank2)
            slots = column_ref[some][:, None]
            total_ref[some] = jnp.where(
                slots == owner_a,
                product[..., :rank2],
                jnp.where(slots == owner_b, product[..., rank2:], total_ref[some]),
            )
            return carry

        if first != peers - 2:
            lax.fori_loop(0, half // group, multiply, 0)
            continue
        for block in reversed(range(half // group)):
            multiply(block, 0)
            for mask in range(block * group, (block + 1) * group):
                if mask:
                    part_ref[mask] = total_ref[mask].astype(jnp.bfloat16)
                    part_copies[mask] = remote(
                        part_ref.at[mask], back_ref.at[mask], part_send, part_recv, mask
                    )
                    part_copies[mask].start()
                    sends.append(part_copies[mask])

    result = total_ref[0]
    for mask in range(1, half):
        part_copies[mask].wait_recv()
        result = result + back_ref[mask].astype(jnp.float32)
    out_ref[...] = result.astype(jnp.bfloat16)
    for copy in sends:
        copy.wait_send()


def low_rank_call(hidden, bank_down, slots, peers):
    bits = peers.bit_length() - 1
    half = peers // 2
    steps_n, rows_here, width = hidden.shape
    chunk = width // half
    rank2 = bank_down.shape[2]
    dma = pltpu.SemaphoreType.DMA
    return pl.pallas_call(
        functools.partial(low_rank_kernel, bits),
        out_shape=jax.ShapeDtypeStruct((steps_n, rows_here, rank2), jnp.bfloat16),
        in_specs=[
            pl.BlockSpec(memory_space=pl.ANY),
            pl.BlockSpec(memory_space=pl.ANY),
            pl.BlockSpec(memory_space=pltpu.VMEM),
        ],
        out_specs=pl.BlockSpec(memory_space=pltpu.VMEM),
        scratch_shapes=[
            pltpu.VMEM((half, steps_n, rows_here, chunk), jnp.bfloat16),
            pltpu.VMEM((peers, chunk, rank2), jnp.bfloat16),
            pltpu.VMEM((half, *slots.shape), jnp.int32),
            pltpu.VMEM((half, rows_here, rank2), jnp.int32),
            pltpu.VMEM((half, steps_n, rows_here, rank2), jnp.float32),
            pltpu.VMEM((half, steps_n, rows_here, rank2), jnp.bfloat16),
            pltpu.VMEM((half, steps_n, rows_here, rank2), jnp.bfloat16),
            dma((2,)),
            dma((half,)),
            dma((half,)),
            dma((half,)),
            dma((half,)),
            dma((peers,)),
            dma((peers,)),
            dma((half,)),
            dma((half,)),
        ],
        compiler_params=pltpu.CompilerParams(
            collective_id=0, has_side_effects=True, vmem_limit_bytes=60 * 1024 * 1024
        ),
        cost_estimate=pl.CostEstimate(
            flops=2 * half * steps_n * rows_here * chunk * peers * rank2,
            bytes_accessed=16 * 1024 * 1024,
            transcendentals=0,
        ),
    )(hidden, bank_down, slots)


def split_width(
    hidden,
    q_base,
    kv_base,
    cache,
    lengths,
    tenant,
    slot_of_tenant,
    bank_down,
    adapter_query_up_stack,
    adapter_key_up_stack,
):
    peers = lax.axis_size("rows")
    steps_n, rows_here, _ = hidden.shape
    head_dim = cache.shape[2] // 2
    width_q = q_base.shape[2]
    rank = adapter_query_up_stack.shape[1]
    tenant_ids = jnp.arange(slot_of_tenant.shape[0], dtype=jnp.int32)
    owner = jnp.sum(
        jnp.where(tenant[:, None] == tenant_ids[None, :], slot_of_tenant[None, :], 0), axis=1
    )
    ups = jnp.concatenate([adapter_query_up_stack[0], adapter_key_up_stack[0]], axis=1)
    ups = lax.all_gather(ups, "rows", axis=0, tiled=True)
    slots = jnp.broadcast_to(owner[None, :], (8, rows_here)).astype(jnp.int32)
    low_rank = low_rank_call(hidden, bank_down, slots, peers)
    chosen = owner[:, None] == jnp.arange(peers, dtype=jnp.int32)[None, :]

    def correction(part, up):
        placed = jnp.where(chosen[None, :, :, None], part[:, :, None, :], 0)
        placed = placed.reshape(steps_n * rows_here, peers * rank).astype(jnp.bfloat16)
        product = jnp.dot(placed, up, preferred_element_type=jnp.float32).astype(jnp.bfloat16)
        return product.astype(jnp.float32).reshape(steps_n, rows_here, up.shape[1])

    delta_q = correction(low_rank[..., :rank], ups[:, :width_q])
    delta_k = correction(low_rank[..., rank:], ups[:, width_q:])
    query = (q_base.astype(jnp.float32) + delta_q).astype(jnp.bfloat16)
    new_key = (kv_base[..., :head_dim].astype(jnp.float32) + delta_k).astype(jnp.bfloat16)
    new_value = kv_base[..., head_dim:]
    return attend(query, new_key, new_value, cache[..., :head_dim], cache[..., head_dim:], lengths)


def local(
    hidden,
    q_base,
    kv_base,
    cache,
    lengths,
    tenant,
    slot_of_tenant,
    bank_down,
    adapter_query_up_stack,
    adapter_key_up_stack,
):
    peer_count = lax.axis_size("rows")
    steps_n, rows_here, model_width = hidden.shape
    capacity = max(2, (2 * rows_here + peer_count - 1) // peer_count)
    tenant_count = slot_of_tenant.shape[0]
    head_dim = cache.shape[2] // 2
    width_q = q_base.shape[2]
    rank_extent = adapter_query_up_stack.shape[1]
    tenant_ids = jnp.arange(tenant_count, dtype=jnp.int32)
    owner_dev = jnp.sum(
        jnp.where(tenant[:, None] == tenant_ids[None, :], slot_of_tenant[None, :], 0), axis=1
    )
    positions = jnp.arange(rows_here, dtype=jnp.int32)
    earlier = (tenant[:, None] == tenant[None, :]) & (positions[None, :] < positions[:, None])
    slot_column = owner_dev * capacity + jnp.sum(earlier.astype(jnp.int32), axis=1)
    placing = (
        slot_column[:, None] == jnp.arange(peer_count * capacity, dtype=jnp.int32)[None, :]
    ).astype(jnp.bfloat16)
    down_projected = bank_down[0]
    up_query = adapter_query_up_stack[0]
    up_key = adapter_key_up_stack[0]
    collected = []
    for step_index in range(steps_n):
        outgoing = jnp.einsum(
            "bc,bd->cd", placing, hidden[step_index], preferred_element_type=jnp.float32
        ).astype(jnp.bfloat16)
        outgoing = outgoing.reshape(peer_count, capacity, model_width)
        received = lax.all_to_all(outgoing, "rows", split_axis=0, concat_axis=0, tiled=True)
        flattened = received.reshape(-1, model_width)
        reduced_rank_input = jnp.dot(
            flattened, down_projected, preferred_element_type=jnp.float32
        ).astype(jnp.bfloat16)
        query_correction = jnp.dot(
            reduced_rank_input[:, :rank_extent], up_query, preferred_element_type=jnp.float32
        ).astype(jnp.bfloat16)
        key_correction = jnp.dot(
            reduced_rank_input[:, rank_extent:], up_key, preferred_element_type=jnp.float32
        ).astype(jnp.bfloat16)
        joined_delta = jnp.concatenate([query_correction, key_correction], axis=1)
        returned = lax.all_to_all(
            joined_delta.reshape(received.shape[0], received.shape[1], width_q + head_dim),
            "rows",
            split_axis=0,
            concat_axis=0,
            tiled=True,
        )
        returned = returned.reshape(peer_count * capacity, width_q + head_dim)
        collected.append(jnp.dot(placing, returned, preferred_element_type=jnp.float32))
    deltas = jnp.stack(collected)
    query = (q_base.astype(jnp.float32) + deltas[..., :width_q]).astype(jnp.bfloat16)
    new_key = (kv_base[..., :head_dim].astype(jnp.float32) + deltas[..., width_q:]).astype(
        jnp.bfloat16
    )
    new_value = kv_base[..., head_dim:]
    return attend(query, new_key, new_value, cache[..., :head_dim], cache[..., head_dim:], lengths)


def solution(mesh):
    peers = mesh.shape["rows"]
    small = 4 <= peers <= 16 and peers & (peers - 1) == 0
    return jax.shard_map(
        split_width if small else local,
        mesh=mesh,
        in_specs=(
            P(None, ("groups", "rows"), None),
            P(None, ("groups", "rows"), None),
            P(None, ("groups", "rows"), None),
            P(("groups", "rows"), None, None),
            P(("groups", "rows")),
            P(("groups", "rows")),
            P("groups"),
            P(("groups", "rows"), None, None),
            P(("groups", "rows"), None, None),
            P(("groups", "rows"), None, None),
        ),
        out_specs=P(None, ("groups", "rows"), None),
        check_vma=False,
    )
```
